32 devices in a mesh: ctx: 8 (over y, x, core), ch: 4 (over z).
Axes of the slice: x: 2, y: 2, z: 4, core: 2. Of those that a mesh axis runs over, the one named last changes fastest.
Arguments:
- query_proj: bfloat16 [2048, 4096], P('ctx', 'ch'), may hold values from -6 to 6
- key_proj: bfloat16 [2048, 4096], P('ctx', 'ch'), may hold values from -6 to 6
- value_proj: bfloat16 [2048, 4096], P('ctx', 'ch'), may hold values from -6 to 6
- filter_in: float32 [33, 64], replicated, may hold values from -3 to 3
- filter_bias: float32 [64], replicated, may hold values from -3.140625 to 3.140625
- filter_out: float32 [64, 256], P(None, 'ch'), may hold values from -0.015625 to 0.015625
- decay_rates: float32 [256], P('ch'), may hold values from 9.765625e-05 to 0.0333333333
- skip_gain: float32 [4096], P('ch'), may hold values from -4 to 4
- out_weight: bfloat16 [4096, 4096], P('ch', 'ctx'), may hold values from -0.125 to 0.125
Outputs:
- layer_out: bfloat16 [2048, 4096], P('ctx', 'ch')
The draws below stay inside these ranges and needn't reach their ends.
All inputs are finite; a program needn't handle non-finite values.
Results may differ from the reference program's by a relative error of at most 0.012.
Values may be sent and summed in bfloat16 or wider, within the bound.
No kernel may reach another device: no remote copies, remote signals or barrier semaphores. Data moves between devices by JAX's collectives and lax.ppermute only.
A program may use at most 128 MiB of HBM per device.

```python
import math
import jax
import jax.numpy as jnp
from jax import lax

D = 4096
GROUP = 16
FEAT = 33
ORDER = 64
SEQ = 2048
GROUPS = 256


def draw_decay_rates(key, part):
    key = jax.random.fold_in(key, 7)
    first_key, second_key, third_key = jax.random.split(key, 3)
    slow_share = 0.5
    slow_rates = jnp.exp(jax.random.uniform(first_key, (GROUPS,), jnp.float32, math.log(0.2 / SEQ), math.log(2.0 / SEQ)))
    fast_rates = jnp.exp(jax.random.uniform(second_key, (GROUPS,), jnp.float32, math.log(1.0 / 50), math.log(1.0 / 30)))
    picked = jax.random.uniform(third_key, (GROUPS,), jnp.float32) < slow_share
    return jnp.where(picked, slow_rates, fast_rates).astype(jnp.float32)


def spiked(result, key, source, target, parts, factor):
    owner, partner = [(jnp.arange(result.shape[dim]) // (result.shape[dim] // parts)).reshape([-1 if axis == dim else 1 for axis in range(result.ndim)]) for dim in (source, target)]
    chosen = jax.random.permutation(key, parts)[partner]
    strong = (owner == chosen) | (owner == (partner + parts // 2) % parts)
    return jnp.where(strong, factor * result, result)


def block_scale(own_key, shape, shards, low, high):
    def one(axis_at, shards_of):
        steps = jax.random.uniform(jax.random.fold_in(jax.random.fold_in(own_key, 6), axis_at), (shards_of,), jnp.float32, low / len(shards), high / len(shards))
        return jnp.repeat(jnp.exp(steps), shape[axis_at] // shards_of).reshape((-1,) + (1,) * (len(shape) - axis_at - 1))

    loudness = one(*shards[0])
    for cut in shards[1:]:
        loudness = loudness * one(*cut)
    return loudness


def noise(key, extent, width, limit, pieces=(), held_as=jnp.bfloat16):
    drawn = width * jax.random.normal(key, extent, jnp.float32)
    if pieces:
        drawn = drawn * block_scale(key, extent, pieces, -0.22, 0.18)
    return jnp.clip(drawn, -limit, limit).astype(held_as)


def bell_draw_with(own_key, extent, spread, reach, cuts, heavy, kind=jnp.bfloat16):
    drawn = spread * jax.random.normal(own_key, extent, jnp.float32)
    if cuts:
        drawn = drawn * block_scale(own_key, extent, cuts, -0.22, 0.18)
    return jnp.clip(spiked(drawn, jax.random.fold_in(own_key, 3), *heavy), -reach, reach).astype(kind)


def setup_inputs(seed: int = 0) -> dict:
    seeds = jax.random.split(jax.random.key(seed), 10)
    query_proj = noise(seeds[0], (SEQ, D), 1.0, 6.0, ((0, 8), (1, 4)))
    key_proj = noise(seeds[1], (SEQ, D), 1.0, 6.0, ((0, 8), (1, 4)))
    value_proj = noise(seeds[2], (SEQ, D), 1.0, 6.0, ((0, 8), (1, 4)))
    filter_in = noise(seeds[3], (FEAT, ORDER), 0.5, 3.0, (), jnp.float32)
    filter_bias = jnp.clip(jax.random.uniform(seeds[4], (ORDER,), jnp.float32, -3.140625, 3.140625), -3.140625, 3.140625)
    filter_out = noise(seeds[5], (ORDER, GROUPS), (ORDER * SEQ) ** -0.5, 0.015625, ((1, 4),), jnp.float32)
    decay_rates = draw_decay_rates(jax.random.fold_in(seeds[9], 71), 0)
    skip_gain = noise(seeds[7], (D,), 1.0, 4.0, ((0, 4),), jnp.float32)
    out_weight = bell_draw_with(seeds[8], (D, D), D ** -0.5, 0.125, ((0, 4), (1, 8)), (0, 1, 8, 2.0))
    return dict(query_proj=query_proj, key_proj=key_proj, value_proj=value_proj, filter_in=filter_in, filter_bias=filter_bias, filter_out=filter_out, decay_rates=decay_rates, skip_gain=skip_gain, out_weight=out_weight)


def position_features(lag_index, seq_len, band_count):
    clamped = jnp.maximum(lag_index, 0)
    harmonics = jnp.arange(1, band_count + 1, dtype=jnp.int32)
    phases = ((clamped[:, None] * harmonics[None, :]) % seq_len).astype(jnp.float32) * (2.0 * math.pi / seq_len)
    ramp_term = (clamped.astype(jnp.float32) / seq_len)[:, None]
    return jnp.concatenate([ramp_term, jnp.cos(phases), jnp.sin(phases)], axis=1)


def filter_values(lag_index, seq_len, filter_in, filter_bias, filter_out, decay_rates):
    band_count = (filter_in.shape[0] - 1) // 2
    features = position_features(lag_index, seq_len, band_count)
    hidden = jnp.sin(jnp.dot(features, filter_in, precision=lax.Precision.HIGHEST, preferred_element_type=jnp.float32) + filter_bias)
    raw_values = jnp.dot(hidden, filter_out, precision=lax.Precision.HIGHEST, preferred_element_type=jnp.float32)
    clamped = jnp.maximum(lag_index, 0).astype(jnp.float32)
    shaped = raw_values * jnp.exp(-decay_rates[None, :] * clamped[:, None])
    return jnp.where((lag_index >= 0)[:, None], shaped, jnp.zeros((), jnp.float32)).astype(jnp.bfloat16)


def reference(query_proj, key_proj, value_proj, filter_in, filter_bias, filter_out, decay_rates, skip_gain, out_weight):
    conv_input = (key_proj.astype(jnp.float32) * value_proj.astype(jnp.float32)).astype(jnp.bfloat16)
    lag_index = jnp.arange(SEQ, dtype=jnp.int32)
    group_filters = filter_values(lag_index, SEQ, filter_in, filter_bias, filter_out, decay_rates)
    per_channel = jnp.repeat(group_filters, GROUP, axis=1)
    block_width = math.gcd(D, 256)
    block_total = D // block_width
    input_blocks = conv_input.astype(jnp.float32).reshape(SEQ, block_total, block_width).transpose(1, 0, 2)
    filter_blocks = per_channel.astype(jnp.float32).reshape(SEQ, block_total, block_width).transpose(1, 0, 2)

    def conv_block(inputs_pair):
        signal, kernel = inputs_pair
        spectrum = jnp.fft.rfft(signal, n=2 * SEQ, axis=0) * jnp.fft.rfft(kernel, n=2 * SEQ, axis=0)
        return jnp.fft.irfft(spectrum, n=2 * SEQ, axis=0)[:SEQ].astype(jnp.float32)

    convolved = lax.map(conv_block, (input_blocks, filter_blocks)).transpose(1, 0, 2).reshape(SEQ, D)
    gated_out = (query_proj.astype(jnp.float32) * (convolved + skip_gain[None, :] * conv_input.astype(jnp.float32))).astype(jnp.bfloat16)
    return jnp.dot(gated_out, out_weight, preferred_element_type=jnp.float32).astype(jnp.bfloat16)
```

```python
import functools
import math

import jax
import jax.numpy as jnp
from jax import lax
from jax.experimental import pallas as pl
from jax.experimental.pallas import tpu as pltpu
from jax.sharding import PartitionSpec as P

BF = jnp.bfloat16
F32 = jnp.float32
LANE = 128
SUB = 16
PARAMS = pltpu.CompilerParams(vmem_limit_bytes=48 * 1024 * 1024)


def pre_kernel(k_ref, v_ref, o_ref):
    prod = k_ref[...].astype(F32) * v_ref[...].astype(F32)
    o_ref[...] = prod.T.astype(BF)


def taps_kernel(seq, me_ref, fin_ref, bias_ref, fout_ref, decay_ref, o_ref):
    bands = (fin_ref.shape[0] - 1) // 2
    groups = o_ref.shape[0]
    all_groups = fout_ref.shape[1]
    contract = functools.partial(
        lax.dot_general, precision=lax.Precision.HIGHEST, preferred_element_type=F32
    )
    first = (((0,), (0,)), ((), ()))
    harmonic = lax.broadcasted_iota(jnp.int32, (bands, seq), 0) + 1
    lag = lax.broadcasted_iota(jnp.int32, (bands, seq), 1)
    phase = lax.rem(harmonic * lag, seq).astype(F32) * (2.0 * math.pi / seq)
    time = lax.broadcasted_iota(jnp.int32, (1, seq), 1).astype(F32)
    pre = contract(fin_ref[1 : 1 + bands, :], jnp.cos(phase), first)
    pre += contract(fin_ref[1 + bands : 1 + 2 * bands, :], jnp.sin(phase), first)
    pre += contract(fin_ref[0:1, :], time / seq, first)
    pre += contract(bias_ref[...], jnp.ones((1, seq), F32), first)
    hidden = jnp.sin(pre)
    row = lax.broadcasted_iota(jnp.int32, (groups, all_groups), 0)
    col = lax.broadcasted_iota(jnp.int32, (groups, all_groups), 1)
    pick = (col == me_ref[0] * groups + row).astype(F32)
    fout = contract(pick, fout_ref[...], (((1,), (1,)), ((), ())))
    decay = jnp.sum(pick * decay_ref[...], axis=1, keepdims=True)
    raw = contract(fout, hidden, (((1,), (0,)), ((), ())))
    o_ref[:, :LANE] = jnp.zeros((groups, LANE), F32)
    o_ref[:, LANE:] = (raw * jnp.exp(-decay * time)).astype(BF).astype(F32)


def conv_kernel(seq, width, taps_ref, u_ref, o_ref, toep, lhs):
    blocks = seq // LANE
    per = u_ref.shape[2] // LANE
    groups = taps_ref.shape[0]
    lhs[...] = jnp.zeros_like(lhs)

    def one(g, carry):
        at = pl.multiple_of(g * width, width)
        line = jnp.broadcast_to(taps_ref[pl.ds(g, 1), :], (SUB, LANE + seq))
        slab = pltpu.roll(line, 0, 1, stride=1, stride_axis=0)
        for k in range(LANE // SUB):
            part = (slab if k == 0 else pltpu.roll(slab, SUB * k, 1)).astype(BF)
            for d in range(blocks):
                toep[LANE * d + SUB * k : LANE * d + SUB * (k + 1), :] = part[
                    :, LANE * (d + 1) : LANE * (d + 2)
                ]
        for b in range(blocks):
            for d in range(b + 1):
                a = b - d
                lhs[width * b : width * (b + 1), LANE * d : LANE * (d + 1)] = u_ref[
                    a // per, pl.ds(at, width), LANE * (a % per) : LANE * (a % per + 1)
                ]
        out = jnp.dot(lhs[...], toep[...], preferred_element_type=F32).astype(BF)
        for b in range(blocks):
            o_ref[b // per, pl.ds(at, width), LANE * (b % per) : LANE * (b % per + 1)] = out[
                width * b : width * (b + 1), :
            ]
        return carry

    lax.fori_loop(0, groups, one, 0)


def gate_kernel(q_ref, k_ref, v_ref, skip_ref, conv_ref, o_ref):
    u = (k_ref[...].astype(F32) * v_ref[...].astype(F32)).astype(BF).astype(F32)
    conv = conv_ref[...].astype(F32).T
    o_ref[...] = (q_ref[...].astype(F32) * (conv + skip_ref[...] * u)).astype(BF)


def project_kernel(sets, ctx_count, ch_count, place_ref, x_ref, *refs):
    weights, (keep_ref, send_ref) = refs[:-2], refs[-2:]
    me, z = place_ref[0], place_ref[1]
    share = ctx_count // ch_count
    for rel in range(ctx_count):
        total = None
        for ref, part in zip(weights, sets):
            for slot, (offset, start, size) in enumerate(part):
                if offset == rel:
                    term = jnp.dot(
                        x_ref[:, start : start + size],
                        ref[slot],
                        preferred_element_type=F32,
                    )
                    total = term if total is None else total + term
        total = total.astype(BF)
        owner = jnp.bitwise_xor(me, rel)
        r = jnp.bitwise_xor(owner // share, z)
        h = owner % share

        @pl.when(r % 2 == 0)
        def _():
            keep_ref[r // 2, h] = total

        @pl.when(r % 2 == 1)
        def _():
            send_ref[r // 2, h] = total


def swap(value, axis, bit):
    count = lax.axis_size(axis)
    return lax.ppermute(value, axis, [(i, i ^ bit) for i in range(count)])


def gather_half(piece, start, bits):
    held = piece[None]
    note = [(0, start, piece.shape[0])]
    for bit in bits[:-1]:
        held = jnp.concatenate([held, swap(held, "ctx", bit)], 0)
        note = note + [(o ^ bit, s, n) for o, s, n in note]
    last = bits[-1]
    return [(held, note), (swap(held, "ctx", last), [(o ^ last, s, n) for o, s, n in note])]


def local(
    query_proj,
    key_proj,
    value_proj,
    filter_in,
    filter_bias,
    filter_out,
    decay_rates,
    skip_gain,
    out_weight,
):
    ctx_count = lax.axis_size("ctx")
    ch_count = lax.axis_size("ch")
    rows, channels = query_proj.shape
    seq = rows * ctx_count
    groups_dev = filter_out.shape[1]
    width = channels // groups_dev
    own = channels // ctx_count
    depth, columns = out_weight.shape
    me = lax.axis_index("ctx")
    z = lax.axis_index("ch")
    place = jnp.stack([me, z]).astype(jnp.int32)
    smem = pl.BlockSpec(memory_space=pltpu.SMEM)
    vmem = pl.BlockSpec(memory_space=pltpu.VMEM)

    u_t = pl.pallas_call(
        pre_kernel,
        out_shape=jax.ShapeDtypeStruct((channels, rows), BF),
        compiler_params=PARAMS,
    )(key_proj, value_proj)
    taps = pl.pallas_call(
        functools.partial(taps_kernel, seq),
        out_shape=jax.ShapeDtypeStruct((own // width, LANE + seq), F32),
        in_specs=[smem] + [vmem] * 4,
        compiler_params=PARAMS,
    )(place, filter_in, filter_bias[None], filter_out, decay_rates[None])
    u_all = lax.all_to_all(u_t.reshape(ctx_count, own, rows), "ctx", 0, 0)
    conv_all = pl.pallas_call(
        functools.partial(conv_kernel, seq, width),
        out_shape=jax.ShapeDtypeStruct(u_all.shape, BF),
        scratch_shapes=[
            pltpu.VMEM((seq, LANE), BF),
            pltpu.VMEM((seq // LANE * width, seq), BF),
        ],
        compiler_params=PARAMS,
    )(taps, u_all)
    conv_t = lax.all_to_all(conv_all, "ctx", 0, 0).reshape(channels, rows)
    gated = pl.pallas_call(
        gate_kernel,
        out_shape=jax.ShapeDtypeStruct((rows, channels), BF),
        compiler_params=PARAMS,
    )(query_proj, key_proj, value_proj, skip_gain[None], conv_t)

    bits = [1 << i for i in range(1, ctx_count.bit_length() - 1)]
    chunk = max(LANE, columns // 2)
    share = ctx_count // ch_count
    results = []
    for at in range(0, columns, chunk):
        part = out_weight[:, at : at + chunk]
        half = depth // 2
        held = gather_half(part[:half], 0, bits + [1]) + gather_half(
            part[half:], half, bits[::-1] + [1]
        )
        keep, send = pl.pallas_call(
            functools.partial(project_kernel, [n for _, n in held], ctx_count, ch_count),
            out_shape=[jax.ShapeDtypeStruct((ch_count // 2, share, rows, chunk), BF)] * 2,
            in_specs=[smem] + [vmem] * (1 + len(held)),
            compiler_params=PARAMS,
        )(place, gated, *[w for w, _ in held])
        bit = 1
        while True:
            got = swap(send, "ch", bit)
            total = keep.astype(F32) + got.astype(F32)
            bit *= 2
            if bit == ch_count:
                break
            keep, send = total[0::2], total[1::2].astype(BF)
        results.append(total[0].astype(BF))
    whole = jnp.stack(results, 0)
    return whole.transpose(2, 1, 0, 3).reshape(rows, share * columns)


def solution(mesh):
    placed = (
        P("ctx", "ch"),
        P("ctx", "ch"),
        P("ctx", "ch"),
        P(),
        P(),
        P(None, "ch"),
        P("ch"),
        P("ch"),
        P("ch", "ctx"),
    )
    return jax.shard_map(
        local, mesh=mesh, in_specs=placed, out_specs=P("ctx", "ch"), check_vma=False
    )
```

```python
import functools
import math

import jax
import jax.numpy as jnp
from jax import lax
from jax.experimental import pallas as pl
from jax.experimental.pallas import tpu as pltpu
from jax.sharding import PartitionSpec as P

BF = jnp.bfloat16
F32 = jnp.float32
LANE = 128
SUB = 16
CHUNK = 256
FULL = pltpu.CompilerParams(vmem_limit_bytes=64 * 1024 * 1024)
PARAMS = pltpu.CompilerParams(vmem_limit_bytes=48 * 1024 * 1024)
SMEM = pl.BlockSpec(memory_space=pltpu.SMEM)
VMEM = pl.BlockSpec(memory_space=pltpu.VMEM)
ANY = pl.BlockSpec(memory_space=pl.ANY)
HBM = pl.BlockSpec(memory_space=pltpu.HBM)
DMA = pltpu.SemaphoreType.DMA


def sine(x):
    n = jnp.round(x * (1.0 / math.pi))
    r = x - n * 3.140625
    r = r - n * 9.67502593994140625e-4
    r = r - n * 1.509957990978376432e-7
    s = r * r
    p = jnp.float32(2.6083159809786593541503e-06)
    p = p * s - 1.981069071916863322258e-04
    p = p * s + 8.33307858556509017944336e-03
    p = p * s - 1.66666597127914428710938e-01
    y = r + r * (s * p)
    return jnp.where((n.astype(jnp.int32) & 1) == 1, -y, y)


def first_kernel(k_hbm, v_hbm, u_hbm, k_ref, v_ref, u_ref, sems, done):
    steps = sems.shape[0]
    part = k_hbm.shape[1] // steps
    spans = [slice(part * i, part * (i + 1)) for i in range(steps)]
    loads = []
    for i, at in enumerate(spans):
        loads.append(pltpu.make_async_copy(k_hbm.at[:, at], k_ref.at[:, at], sems.at[i, 0]))
        loads.append(pltpu.make_async_copy(v_hbm.at[:, at], v_ref.at[:, at], sems.at[i, 1]))
    for load in loads:
        load.start()
    stores = []
    for i, at in enumerate(spans):
        loads[2 * i].wait()
        loads[2 * i + 1].wait()
        prod = k_ref[:, at].astype(F32) * v_ref[:, at].astype(F32)
        u_ref[at, :] = prod.T.astype(BF)
        stores.append(pltpu.make_async_copy(u_ref.at[at], u_hbm.at[at], done.at[i]))
        stores[i].start()
    for store in stores:
        store.wait()


def taps_kernel(
    seq, me_ref, fin_hbm, bias_hbm, fout_hbm, decay_hbm, w_hbm, u_hbm, o_ref, *rest
):
    cuts, held, sems, cut_sems = rest[:-6], rest[-6:-2], rest[-2], rest[-1]
    moves, at = [], 0
    for n, cut in enumerate(cuts):
        half, size = cut.shape[1:]
        for m in range(2):
            source = w_hbm.at[pl.ds(half * m, half), pl.ds(at, size)]
            moves.append(pltpu.make_async_copy(source, cut.at[m], cut_sems.at[n, m]))
        at += size
    loads = [
        pltpu.make_async_copy(source, target, sems.at[i])
        for i, (source, target) in enumerate(zip((fin_hbm, bias_hbm, fout_hbm, decay_hbm), held))
    ]
    for load in loads + moves:
        load.start()
    for load in loads:
        load.wait()
    fin_ref, bias_ref, fout_ref, decay_ref = held
    bands = (fin_ref.shape[0] - 1) // 2
    groups = o_ref.shape[0]
    all_groups = fout_ref.shape[1]
    contract = functools.partial(
        lax.dot_general, precision=lax.Precision.HIGHEST, preferred_element_type=F32
    )
    first = (((0,), (0,)), ((), ()))
    harmonic = lax.broadcasted_iota(jnp.int32, (bands, seq), 0) + 1
    lag = lax.broadcasted_iota(jnp.int32, (bands, seq), 1)
    phase = lax.rem(harmonic * lag, seq).astype(F32) * (2.0 * math.pi / seq)
    time = lax.broadcasted_iota(jnp.int32, (1, seq), 1).astype(F32)
    pre = contract(fin_ref[1 : 1 + bands, :], sine(phase + math.pi / 2), first)
    pre += contract(fin_ref[1 + bands : 1 + 2 * bands, :], sine(phase), first)
    pre += contract(fin_ref[0:1, :], time / seq, first)
    pre += contract(bias_ref[...], jnp.ones((1, seq), F32), first)
    hidden = sine(pre)
    row = lax.broadcasted_iota(jnp.int32, (groups, all_groups), 0)
    col = lax.broadcasted_iota(jnp.int32, (groups, all_groups), 1)
    pick = (col == me_ref[0] * groups + row).astype(F32)
    fout = contract(pick, fout_ref[...], (((1,), (1,)), ((), ())))
    decay = jnp.sum(pick * decay_ref[...], axis=1, keepdims=True)
    raw = contract(fout, hidden, (((1,), (0,)), ((), ())))
    o_ref[:, :LANE] = jnp.zeros((groups, LANE), F32)
    o_ref[:, LANE:] = (raw * jnp.exp(-decay * time)).astype(BF).astype(F32)
    for move in moves:
        move.wait()


def conv_kernel(seq, width, taps_ref, u_hbm, o_hbm, rev, toep, out_ref, sems, done):
    blocks = seq // LANE
    per = u_hbm.shape[2] // LANE
    groups = taps_ref.shape[0]
    loads = []
    for a in range(blocks):
        source = u_hbm.at[a // per, :, pl.ds(LANE * (a % per), LANE)]
        target = rev.at[:, pl.ds(LANE * (blocks - 1 - a), LANE)]
        loads.append(pltpu.make_async_copy(source, target, sems.at[a]))
        loads[a].start()
    rev[:, seq:] = jnp.zeros((rev.shape[0], rev.shape[1] - seq), BF)
    stores = []
    for g in range(groups):
        line = jnp.broadcast_to(taps_ref[g : g + 1, :], (SUB, LANE + seq))
        slab = pltpu.roll(line, 0, 1, stride=1, stride_axis=0)
        for k in range(LANE // SUB):
            part = (slab if k == 0 else pltpu.roll(slab, SUB * k, 1)).astype(BF)
            for d in range(blocks):
                toep[g % 2, LANE * d + SUB * k : LANE * d + SUB * (k + 1), :] = part[
                    :, LANE * (d + 1) : LANE * (d + 2)
                ]
        if g == 0:
            for load in loads:
                load.wait()
        mine = slice(width * g, width * (g + 1))
        starts = [LANE * (blocks - 1 - b) for b in range(blocks)]
        lhs = jnp.concatenate([rev[mine, at : at + seq] for at in starts], 0)
        out = jnp.dot(lhs, toep[g % 2], preferred_element_type=F32).astype(BF)
        for b in range(blocks):
            out_ref[b // per, mine, LANE * (b % per) : LANE * (b % per + 1)] = out[
                width * b : width * (b + 1), :
            ]
        stores.append(
            pltpu.make_async_copy(out_ref.at[:, mine], o_hbm.at[:, mine], done.at[g])
        )
        stores[g].start()
    for store in stores:
        store.wait()


def gate_kernel(q_hbm, k_hbm, v_hbm, skip_hbm, conv_hbm, o_ref, q_ref, k_ref, v_ref, skip_ref, conv_ref, sems):
    steps = sems.shape[0]
    part = q_hbm.shape[1] // steps
    spans = [slice(part * i, part * (i + 1)) for i in range(steps)]
    pairs = ((q_hbm, q_ref), (k_hbm, k_ref), (v_hbm, v_ref), (skip_hbm, skip_ref))
    loads = []
    for i, at in enumerate(spans):
        step = [pltpu.make_async_copy(conv_hbm.at[at], conv_ref.at[at], sems.at[i, 4])]
        for n, (source, target) in enumerate(pairs):
            step.append(pltpu.make_async_copy(source.at[:, at], target.at[:, at], sems.at[i, n]))
        for load in step:
            load.start()
        loads.append(step)
    for i, at in enumerate(spans):
        for load in loads[i]:
            load.wait()
        u = (k_ref[:, at].astype(F32) * v_ref[:, at].astype(F32)).astype(BF).astype(F32)
        conv = conv_ref[at, :].astype(F32).T
        gated = q_ref[:, at].astype(F32) * (conv + skip_ref[:, at] * u)
        o_ref[:, at] = gated.astype(BF)


def block_kernel(r, place_ref, x_ref, y_ref, own_ref, by_x_ref, by_y_ref, far_0_ref, far_1_ref, o_ref, held, sems):
    half = held.shape[0] // 2
    rows = x_ref.shape[0]
    chip = jnp.bitwise_xor(jnp.bitwise_xor(place_ref[1], r), place_ref[0] // 2)
    sources = [(own_ref.at[0], own_ref.at[1]), (by_x_ref.at[0], by_x_ref.at[1])]
    sources += [(by_y_ref.at[0], by_y_ref.at[1]), (far_0_ref.at[0], far_1_ref.at[0])]
    for choice, parts in enumerate(sources):

        @pl.when(chip == choice)
        def _():
            for n, part in enumerate(parts):
                pltpu.make_async_copy(
                    part, held.at[pl.ds(half * n, half)], sems.at[n]
                ).start()

    for n in range(2):
        pltpu.make_async_copy(
            own_ref.at[n], held.at[pl.ds(half * n, half)], sems.at[n]
        ).wait()
    o_ref[:rows] = jnp.dot(x_ref[...], held[...], preferred_element_type=F32).astype(BF)
    o_ref[rows:] = jnp.dot(y_ref[...], held[...], preferred_element_type=F32).astype(BF)


def last_kernel(chunks, place_ref, *refs):
    o_ref = refs[-1]
    core = place_ref[0] % 2
    at = 0
    for n, size in enumerate(chunks):
        for half, ref in ((core, refs[2 * n]), (1 - core, refs[2 * n + 1])):
            to = pl.multiple_of(half * (o_ref.shape[1] // 2) + at, LANE)
            o_ref[:, pl.ds(to, size)] = ref[...]
        at += size


def after_kernel(count, *refs):
    pass


def after(values, *others):
    values = list(values)
    count = len(values)
    return pl.pallas_call(
        functools.partial(after_kernel, count),
        out_shape=[jax.ShapeDtypeStruct(v.shape, v.dtype) for v in values],
        in_specs=[ANY] * (count + len(others)),
        out_specs=[ANY] * count,
        input_output_aliases={i: i for i in range(count)},
        compiler_params=PARAMS,
    )(*values, *others)


def swap(value, axis, bit):
    count = lax.axis_size(axis)
    return lax.ppermute(value, axis, [(i, i ^ bit) for i in range(count)])


def project_pairs(place, gated, cuts, conv_all):
    rows = gated.shape[0]
    call = functools.partial(pl.pallas_call, compiler_params=PARAMS)
    shape = jax.ShapeDtypeStruct
    other = swap(gated, "ctx", 1)
    finals = []
    previous = (conv_all,)
    for number, cut in enumerate(cuts):
        depth, n = 2 * cut.shape[1], cut.shape[2]
        if number:
            (cut,) = after([cut], *gate)
        by_x, by_y = swap(cut, "ctx", 2), swap(cut, "ctx", 4)
        by_x, by_y = after([by_x, by_y], *previous)
        far_1 = swap(by_x[1:], "ctx", 4)
        far_0 = swap(by_y[:1], "ctx", 2)
        gate = (far_0, far_1)
        blocks = {}
        for r in (3, 1, 2, 0):
            blocks[r] = call(
                functools.partial(block_kernel, r),
                out_shape=shape((2 * rows, n), BF),
                in_specs=[SMEM, VMEM, VMEM] + [ANY] * 5,
                scratch_shapes=[
                    pltpu.VMEM((depth, n), BF),
                    pltpu.SemaphoreType.DMA((2,)),
                ],
            )(place, gated, other, cut, by_x, by_y, far_0, far_1)
        got_3 = swap(blocks[3], "ch", 1)
        got_1 = swap(blocks[1], "ch", 1)
        previous = (got_3, got_1)
        two = (blocks[2].astype(F32) + got_3.astype(F32)).astype(BF)
        got_2 = swap(two, "ch", 2)
        total = blocks[0].astype(F32) + got_1.astype(F32) + got_2.astype(F32)
        mine, theirs = total[:rows].astype(BF), total[rows:].astype(BF)
        finals += [mine, swap(theirs, "ctx", 1)]
    return call(
        functools.partial(last_kernel, [c.shape[2] for c in cuts]),
        out_shape=shape((rows, 2 * sum(c.shape[2] for c in cuts)), BF),
        in_specs=[SMEM] + [VMEM] * len(finals),
    )(place, *finals)


def local(
    query_proj,
    key_proj,
    value_proj,
    filter_in,
    filter_bias,
    filter_out,
    decay_rates,
    skip_gain,
    out_weight,
):
    ctx_count = lax.axis_size("ctx")
    ch_count = lax.axis_size("ch")
    rows, channels = query_proj.shape
    seq = rows * ctx_count
    width = channels // filter_out.shape[1]
    own = channels // ctx_count
    depth, columns = out_weight.shape
    pairs = ctx_count == 8 and ch_count == 4
    me = lax.axis_index("ctx")
    z = lax.axis_index("ch")
    place = jnp.stack([me, z]).astype(jnp.int32)
    call = functools.partial(pl.pallas_call, compiler_params=PARAMS)
    shape = jax.ShapeDtypeStruct

    chunks = [CHUNK] * (columns // CHUNK) if pairs else []
    steps = 4
    groups = own // width
    u_t = pl.pallas_call(
        first_kernel,
        compiler_params=FULL,
        out_shape=shape((channels, rows), BF),
        in_specs=[HBM, HBM],
        out_specs=HBM,
        scratch_shapes=[
            pltpu.VMEM((rows, channels), BF),
            pltpu.VMEM((rows, channels), BF),
            pltpu.VMEM((channels, rows), BF),
            DMA((steps, 2)),
            DMA((steps,)),
        ],
    )(key_proj, value_proj)
    u_all = lax.all_to_all(u_t.reshape(ctx_count, own, rows), "ctx", 0, 0)
    small = (filter_in, filter_bias[None], filter_out, decay_rates[None])
    taps, *cuts = call(
        functools.partial(taps_kernel, seq),
        out_shape=[shape((groups, LANE + seq), F32)]
        + [shape((2, depth // 2, n), BF) for n in chunks],
        in_specs=[SMEM] + [HBM] * 6,
        out_specs=[VMEM] + [HBM] * len(chunks),
        scratch_shapes=[pltpu.VMEM(a.shape, F32) for a in small]
        + [DMA((4,)), DMA((max(1, len(chunks)), 2))],
    )(place, *small, out_weight, u_t)
    conv_all = call(
        functools.partial(conv_kernel, seq, width),
        out_shape=shape(u_all.shape, BF),
        in_specs=[VMEM, HBM],
        out_specs=HBM,
        scratch_shapes=[
            pltpu.VMEM((own, 2 * seq), BF),
            pltpu.VMEM((2, seq, LANE), BF),
            pltpu.VMEM(u_all.shape, BF),
            DMA((seq // LANE,)),
            DMA((groups,)),
        ],
    )(taps, u_all)
    conv_t = lax.all_to_all(conv_all, "ctx", 0, 0).reshape(channels, rows)
    gated = call(
        gate_kernel,
        out_shape=shape((rows, channels), BF),
        in_specs=[HBM] * 5,
        out_specs=VMEM,
        scratch_shapes=[pltpu.VMEM((rows, channels), BF)] * 3
        + [
            pltpu.VMEM((1, channels), F32),
            pltpu.VMEM((channels, rows), BF),
            DMA((steps, 5)),
        ],
    )(query_proj, key_proj, value_proj, skip_gain[None], conv_t)
    if pairs:
        return project_pairs(place, gated, cuts, conv_all)
    everything = lax.all_gather(out_weight, "ctx", axis=1, tiled=True)
    sums = jnp.dot(gated, everything, preferred_element_type=F32).astype(BF)
    return lax.psum_scatter(sums, "ch", scatter_dimension=1, tiled=True)


def solution(mesh):
    placed = (
        P("ctx", "ch"),
        P("ctx", "ch"),
        P("ctx", "ch"),
        P(),
        P(),
        P(None, "ch"),
        P("ch"),
        P("ch"),
        P("ch", "ctx"),
    )
    return jax.shard_map(
        local, mesh=mesh, in_specs=placed, out_specs=P("ctx", "ch"), check_vma=False
    )
```

```python
import functools
import math

import jax
import jax.numpy as jnp
from jax import lax
from jax.experimental import pallas as pl
from jax.experimental.pallas import tpu as pltpu
from jax.sharding import PartitionSpec as P

BF = jnp.bfloat16
F32 = jnp.float32
LANE = 128
SUB = 16
CHUNK = 256
FULL = pltpu.CompilerParams(vmem_limit_bytes=64 * 1024 * 1024)
PARAMS = pltpu.CompilerParams(vmem_limit_bytes=48 * 1024 * 1024)
SMEM = pl.BlockSpec(memory_space=pltpu.SMEM)
VMEM = pl.BlockSpec(memory_space=pltpu.VMEM)
ANY = pl.BlockSpec(memory_space=pl.ANY)
HBM = pl.BlockSpec(memory_space=pltpu.HBM)
DMA = pltpu.SemaphoreType.DMA


def sine(x):
    n = jnp.round(x * (1.0 / math.pi))
    r = x - n * 3.140625
    r = r - n * 9.67502593994140625e-4
    r = r - n * 1.509957990978376432e-7
    s = r * r
    p = jnp.float32(2.6083159809786593541503e-06)
    p = p * s - 1.981069071916863322258e-04
    p = p * s + 8.33307858556509017944336e-03
    p = p * s - 1.66666597127914428710938e-01
    y = r + r * (s * p)
    return jnp.where((n.astype(jnp.int32) & 1) == 1, -y, y)


def first_kernel(k_hbm, v_hbm, u_hbm, k_ref, v_ref, u_ref, sems, done):
    steps = sems.shape[0]
    part = k_hbm.shape[1] // steps
    spans = [slice(part * i, part * (i + 1)) for i in range(steps)]
    loads = []
    for i, at in enumerate(spans):
        loads.append(pltpu.make_async_copy(k_hbm.at[:, at], k_ref.at[:, at], sems.at[i, 0]))
        loads.append(pltpu.make_async_copy(v_hbm.at[:, at], v_ref.at[:, at], sems.at[i, 1]))
    for load in loads:
        load.start()
    stores = []
    for i, at in enumerate(spans):
        loads[2 * i].wait()
        loads[2 * i + 1].wait()
        prod = k_ref[:, at].astype(F32) * v_ref[:, at].astype(F32)
        u_ref[at, :] = prod.T.astype(BF)
        stores.append(pltpu.make_async_copy(u_ref.at[at], u_hbm.at[at], done.at[i]))
        stores[i].start()
    for store in stores:
        store.wait()


def taps_kernel(
    seq, me_ref, fin_hbm, bias_hbm, fout_hbm, decay_hbm, w_hbm, u_hbm, o_ref, *rest
):
    cuts, held, sems, cut_sems = rest[:-6], rest[-6:-2], rest[-2], rest[-1]
    moves, at = [], 0
    for n, cut in enumerate(cuts):
        half, size = cut.shape[1:]
        for m in range(2):
            source = w_hbm.at[pl.ds(half * m, half), pl.ds(at, size)]
            moves.append(pltpu.make_async_copy(source, cut.at[m], cut_sems.at[n, m]))
        at += size
    loads = [
        pltpu.make_async_copy(source, target, sems.at[i])
        for i, (source, target) in enumerate(zip((fin_hbm, bias_hbm, fout_hbm, decay_hbm), held))
    ]
    for load in loads + moves:
        load.start()
    for load in loads:
        load.wait()
    fin_ref, bias_ref, fout_ref, decay_ref = held
    bands = (fin_ref.shape[0] - 1) // 2
    groups = o_ref.shape[0]
    all_groups = fout_ref.shape[1]
    contract = functools.partial(
        lax.dot_general, precision=lax.Precision.HIGHEST, preferred_element_type=F32
    )
    first = (((0,), (0,)), ((), ()))
    harmonic = lax.broadcasted_iota(jnp.int32, (bands, seq), 0) + 1
    lag = lax.broadcasted_iota(jnp.int32, (bands, seq), 1)
    phase = lax.rem(harmonic * lag, seq).astype(F32) * (2.0 * math.pi / seq)
    time = lax.broadcasted_iota(jnp.int32, (1, seq), 1).astype(F32)
    pre = contract(fin_ref[1 : 1 + bands, :], sine(phase + math.pi / 2), first)
    pre += contract(fin_ref[1 + bands : 1 + 2 * bands, :], sine(phase), first)
    pre += contract(fin_ref[0:1, :], time / seq, first)
    pre += contract(bias_ref[...], jnp.ones((1, seq), F32), first)
    hidden = sine(pre)
    row = lax.broadcasted_iota(jnp.int32, (groups, all_groups), 0)
    col = lax.broadcasted_iota(jnp.int32, (groups, all_groups), 1)
    pick = (col == me_ref[0] * groups + row).astype(F32)
    fout = contract(pick, fout_ref[...], (((1,), (1,)), ((), ())))
    decay = jnp.sum(pick * decay_ref[...], axis=1, keepdims=True)
    raw = contract(fout, hidden, (((1,), (0,)), ((), ())))
    taps = (raw * jnp.exp(-decay * time)).astype(BF).astype(F32)
    for g in range(groups):
        line = jnp.concatenate([jnp.zeros((1, LANE), F32), taps[g : g + 1, :]], 1)
        line = jnp.broadcast_to(line, (SUB, LANE + seq))
        o_ref[g] = pltpu.roll(line, 0, 1, stride=1, stride_axis=0).astype(BF)
    for move in moves:
        move.wait()


def conv_kernel(seq, width, taps_ref, u_hbm, o_hbm, rev, toep, out_ref, sems, done):
    blocks = seq // LANE
    per = u_hbm.shape[2] // LANE
    groups = taps_ref.shape[0]
    loads = []
    for a in range(blocks):
        source = u_hbm.at[a // per, :, pl.ds(LANE * (a % per), LANE)]
        target = rev.at[:, pl.ds(LANE * (blocks - 1 - a), LANE)]
        loads.append(pltpu.make_async_copy(source, target, sems.at[a]))
        loads[a].start()
    rev[:, seq:] = jnp.zeros((rev.shape[0], rev.shape[1] - seq), BF)
    stores = []
    for g in range(groups):
        slab = taps_ref[g]
        for k in range(LANE // SUB):
            part = slab if k == 0 else pltpu.roll(slab, SUB * k, 1)
            for d in range(blocks):
                toep[g % 2, LANE * d + SUB * k : LANE * d + SUB * (k + 1), :] = part[
                    :, LANE * (d + 1) : LANE * (d + 2)
                ]
        if g == 0:
            for load in loads:
                load.wait()
        mine = slice(width * g, width * (g + 1))
        starts = [LANE * (blocks - 1 - b) for b in range(blocks)]
        lhs = jnp.concatenate([rev[mine, at : at + seq] for at in starts], 0)
        out = jnp.dot(lhs, toep[g % 2], preferred_element_type=F32).astype(BF)
        for b in range(blocks):
            out_ref[b // per, mine, LANE * (b % per) : LANE * (b % per + 1)] = out[
                width * b : width * (b + 1), :
            ]
        stores.append(
            pltpu.make_async_copy(out_ref.at[:, mine], o_hbm.at[:, mine], done.at[g])
        )
        stores[g].start()
    for store in stores:
        store.wait()


def gate_kernel(q_hbm, u_hbm, skip_hbm, conv_hbm, o_ref, q_ref, u_ref, skip_ref, conv_ref, sems):
    steps = sems.shape[0]
    part = q_hbm.shape[1] // steps
    spans = [slice(part * i, part * (i + 1)) for i in range(steps)]
    loads = []
    for i, at in enumerate(spans):
        step = [
            pltpu.make_async_copy(conv_hbm.at[at], conv_ref.at[at], sems.at[i, 0]),
            pltpu.make_async_copy(u_hbm.at[at], u_ref.at[at], sems.at[i, 1]),
            pltpu.make_async_copy(q_hbm.at[:, at], q_ref.at[:, at], sems.at[i, 2]),
            pltpu.make_async_copy(skip_hbm.at[:, at], skip_ref.at[:, at], sems.at[i, 3]),
        ]
        for load in step:
            load.start()
        loads.append(step)
    for i, at in enumerate(spans):
        for load in loads[i]:
            load.wait()
        u = u_ref[at, :].astype(F32).T
        conv = conv_ref[at, :].astype(F32).T
        gated = q_ref[:, at].astype(F32) * (conv + skip_ref[:, at] * u)
        o_ref[:, at] = gated.astype(BF)


def block_kernel(r, place_ref, x_ref, y_ref, own_ref, by_x_ref, by_y_ref, far_0_ref, far_1_ref, o_ref, held, sems):
    half = held.shape[0] // 2
    rows = x_ref.shape[0]
    chip = jnp.bitwise_xor(jnp.bitwise_xor(place_ref[1], r), place_ref[0] // 2)
    sources = [(own_ref.at[0], own_ref.at[1]), (by_x_ref.at[0], by_x_ref.at[1])]
    sources += [(by_y_ref.at[0], by_y_ref.at[1]), (far_0_ref.at[0], far_1_ref.at[0])]
    for choice, parts in enumerate(sources):

        @pl.when(chip == choice)
        def _():
            for n, part in enumerate(parts):
                pltpu.make_async_copy(
                    part, held.at[pl.ds(half * n, half)], sems.at[n]
                ).start()

    for n in range(2):
        pltpu.make_async_copy(
            own_ref.at[n], held.at[pl.ds(half * n, half)], sems.at[n]
        ).wait()
    o_ref[:rows] = jnp.dot(x_ref[...], held[...], preferred_element_type=F32).astype(BF)
    o_ref[rows:] = jnp.dot(y_ref[...], held[...], preferred_element_type=F32).astype(BF)


def last_kernel(chunks, place_ref, *refs):
    o_ref = refs[-1]
    core = place_ref[0] % 2
    at = 0
    for n, size in enumerate(chunks):
        for half, ref in ((core, refs[2 * n]), (1 - core, refs[2 * n + 1])):
            to = pl.multiple_of(half * (o_ref.shape[1] // 2) + at, LANE)
            o_ref[:, pl.ds(to, size)] = ref[...]
        at += size


def after_kernel(count, *refs):
    pass


def after(values, *others):
    values = list(values)
    count = len(values)
    return pl.pallas_call(
        functools.partial(after_kernel, count),
        out_shape=[jax.ShapeDtypeStruct(v.shape, v.dtype) for v in values],
        in_specs=[ANY] * (count + len(others)),
        out_specs=[ANY] * count,
        input_output_aliases={i: i for i in range(count)},
        compiler_params=PARAMS,
    )(*values, *others)


def swap(value, axis, bit):
    count = lax.axis_size(axis)
    return lax.ppermute(value, axis, [(i, i ^ bit) for i in range(count)])


def project_pairs(place, gated, cuts, conv_all):
    rows = gated.shape[0]
    call = functools.partial(pl.pallas_call, compiler_params=PARAMS)
    shape = jax.ShapeDtypeStruct
    other = swap(gated, "ctx", 1)
    finals = []
    previous = (conv_all,)
    for number, cut in enumerate(cuts):
        depth, n = 2 * cut.shape[1], cut.shape[2]
        if number:
            (cut,) = after([cut], *gate)
        by_x, by_y = swap(cut, "ctx", 2), swap(cut, "ctx", 4)
        by_x, by_y = after([by_x, by_y], *previous)
        far_1 = swap(by_x[1:], "ctx", 4)
        far_0 = swap(by_y[:1], "ctx", 2)
        gate = (far_0, far_1)
        blocks = {}
        for r in (3, 1, 2, 0):
            blocks[r] = call(
                functools.partial(block_kernel, r),
                out_shape=shape((2 * rows, n), BF),
                in_specs=[SMEM, VMEM, VMEM] + [ANY] * 5,
                scratch_shapes=[
                    pltpu.VMEM((depth, n), BF),
                    pltpu.SemaphoreType.DMA((2,)),
                ],
            )(place, gated, other, cut, by_x, by_y, far_0, far_1)
        got_3 = swap(blocks[3], "ch", 1)
        got_1 = swap(blocks[1], "ch", 1)
        previous = (got_3, got_1)
        two = (blocks[2].astype(F32) + got_3.astype(F32)).astype(BF)
        got_2 = swap(two, "ch", 2)
        total = blocks[0].astype(F32) + got_1.astype(F32) + got_2.astype(F32)
        mine, theirs = total[:rows].astype(BF), total[rows:].astype(BF)
        finals += [mine, swap(theirs, "ctx", 1)]
    return call(
        functools.partial(last_kernel, [c.shape[2] for c in cuts]),
        out_shape=shape((rows, 2 * sum(c.shape[2] for c in cuts)), BF),
        in_specs=[SMEM] + [VMEM] * len(finals),
    )(place, *finals)


def local(
    query_proj,
    key_proj,
    value_proj,
    filter_in,
    filter_bias,
    filter_out,
    decay_rates,
    skip_gain,
    out_weight,
):
    ctx_count = lax.axis_size("ctx")
    ch_count = lax.axis_size("ch")
    rows, channels = query_proj.shape
    seq = rows * ctx_count
    width = channels // filter_out.shape[1]
    own = channels // ctx_count
    depth, columns = out_weight.shape
    pairs = ctx_count == 8 and ch_count == 4
    me = lax.axis_index("ctx")
    z = lax.axis_index("ch")
    place = jnp.stack([me, z]).astype(jnp.int32)
    call = functools.partial(pl.pallas_call, compiler_params=PARAMS)
    shape = jax.ShapeDtypeStruct

    chunks = [CHUNK] * (columns // CHUNK) if pairs else []
    steps = 4
    groups = own // width
    u_t = pl.pallas_call(
        first_kernel,
        compiler_params=FULL,
        out_shape=shape((channels, rows), BF),
        in_specs=[HBM, HBM],
        out_specs=HBM,
        scratch_shapes=[
            pltpu.VMEM((rows, channels), BF),
            pltpu.VMEM((rows, channels), BF),
            pltpu.VMEM((channels, rows), BF),
            DMA((steps, 2)),
            DMA((steps,)),
        ],
    )(key_proj, value_proj)
    u_all = lax.all_to_all(u_t.reshape(ctx_count, own, rows), "ctx", 0, 0)
    small = (filter_in, filter_bias[None], filter_out, decay_rates[None])
    taps, *cuts = call(
        functools.partial(taps_kernel, seq),
        out_shape=[shape((groups, SUB, LANE + seq), BF)]
        + [shape((2, depth // 2, n), BF) for n in chunks],
        in_specs=[SMEM] + [HBM] * 6,
        out_specs=[VMEM] + [HBM] * len(chunks),
        scratch_shapes=[pltpu.VMEM(a.shape, F32) for a in small]
        + [DMA((4,)), DMA((max(1, len(chunks)), 2))],
    )(place, *small, out_weight, u_t)
    conv_all = call(
        functools.partial(conv_kernel, seq, width),
        out_shape=shape(u_all.shape, BF),
        in_specs=[VMEM, HBM],
        out_specs=HBM,
        scratch_shapes=[
            pltpu.VMEM((own, 2 * seq), BF),
            pltpu.VMEM((2, seq, LANE), BF),
            pltpu.VMEM(u_all.shape, BF),
            DMA((seq // LANE,)),
            DMA((groups,)),
        ],
    )(taps, u_all)
    conv_t = lax.all_to_all(conv_all, "ctx", 0, 0).reshape(channels, rows)
    gated = call(
        gate_kernel,
        out_shape=shape((rows, channels), BF),
        in_specs=[HBM] * 4,
        out_specs=VMEM,
        scratch_shapes=[
            pltpu.VMEM((rows, channels), BF),
            pltpu.VMEM((channels, rows), BF),
            pltpu.VMEM((1, channels), F32),
            pltpu.VMEM((channels, rows), BF),
            DMA((steps, 4)),
        ],
    )(query_proj, u_t, skip_gain[None], conv_t)
    if pairs:
        return project_pairs(place, gated, cuts, conv_all)
    everything = lax.all_gather(out_weight, "ctx", axis=1, tiled=True)
    sums = jnp.dot(gated, everything, preferred_element_type=F32).astype(BF)
    return lax.psum_scatter(sums, "ch", scatter_dimension=1, tiled=True)


def solution(mesh):
    placed = (
        P("ctx", "ch"),
        P("ctx", "ch"),
        P("ctx", "ch"),
        P(),
        P(),
        P(None, "ch"),
        P("ch"),
        P("ch"),
        P("ch", "ctx"),
    )
    return jax.shard_map(
        local, mesh=mesh, in_specs=placed, out_specs=P("ctx", "ch"), check_vma=False
    )
```
